128 devices in a mesh: seg: 8 (over x, core), sec: 16 (over y, z).
Axes of the slice: x: 4, y: 4, z: 4, core: 2. Of those that a mesh axis runs over, the one named last changes fastest.
Arguments:
- theta_start: float32 [131072], P(('seg', 'sec')), may hold values from 0.8 to 1.2
- reflect: float32 [8, 131072], P(None, ('seg', 'sec')), may hold values from 0.2 to 0.7
- surface: float32 [7, 131072], P(None, ('seg', 'sec')), may hold values from -4 to 4, as said below
- member: int32 [131072], P(('seg', 'sec')), may hold values from 0 to 1023, as said below
- cell_map: int32 [131072], P(('seg', 'sec')), may hold values from 0 to 255
- pairs: int32 [4096, 2], P(('seg', 'sec')), may hold values from 0 to 255, as said below
- counts: int32 [128], P(('seg', 'sec')), may hold values from 8 to 32, as said below
- air_start: float32 [2, 16, 2048], P(None, 'seg', 'sec'), may hold values from -2 to 2
Outputs:
- theta: float32 [131072], P(('seg', 'sec'))
- radiosity: float32 [8, 131072], P(None, ('seg', 'sec'))
- air: float32 [2, 16, 2048], P(None, 'seg', 'sec')
The draws below stay inside these ranges and needn't reach their ends.
Inputs may be any that keep to these rules, and one draw needn't show every extreme that they name: `member`: a permutation of 0 to 1023 on each device. `pairs`: column 0 is 0 to 1; column 1 is a block of another device whose seg index is the owner's or one higher. `counts`: some device holds 32. `surface`: normals have unit length, areas 0.5 to 2.
All inputs are finite; a program needn't handle non-finite values.
Results may differ from the reference program's by a relative error of at most 0.0003.
Values may be sent and summed in bfloat16 or wider, within the bound.
No kernel may reach another device: no remote copies, remote signals or barrier semaphores. Data moves between devices by JAX's collectives and lax.ppermute only.
A program may use at most 128 MiB of HBM per device.

```python
import math
import jax
import jax.numpy as jnp
from jax import lax

BANDS = 8
BLK = 512
NB_DEV = 2
PAIR_DEV = 32
AX = 2
AR = 128
ITERS = 3
PATCHES = 131072
BLOCKS = 256
PAIRS = 4096
NAX = 16
NAR = 2048
N_SEG = 8
N_SEC = 16


def draw_surface(key, part):
    key = jax.random.fold_in(key, 11)
    k_place, k_polar, k_azim, k_area = jax.random.split(key, 4)
    place = jnp.clip(jax.random.normal(k_place, (3, PATCHES)), -4.0, 4.0)
    polar = jax.random.uniform(k_polar, (PATCHES,), minval=-1.0, maxval=1.0)
    azim = jax.random.uniform(k_azim, (PATCHES,), minval=-math.pi, maxval=math.pi)
    sine = jnp.sqrt(jnp.maximum(1.0 - polar * polar, 0.0))
    normal = jnp.stack([sine * jnp.cos(azim), sine * jnp.sin(azim), polar])
    area = jnp.exp(jax.random.uniform(k_area, (1, PATCHES), minval=math.log(0.5), maxval=math.log(2.0)))
    return jnp.concatenate([place, normal, area], 0).astype(jnp.float32)


def draw_member(key, part):
    key = jax.random.fold_in(key, 12)
    keys = jax.random.split(key, N_SEG * N_SEC)
    perms = jax.vmap(lambda k: jax.random.permutation(k, NB_DEV * BLK))(keys)
    return perms.reshape(-1).astype(jnp.int32)


def draw_pairs(key, part):
    key = jax.random.fold_in(key, 13)
    k_local, k_step, k_sector, k_block = jax.random.split(key, 4)
    owner = jnp.arange(PAIRS, dtype=jnp.int32) // PAIR_DEV
    seg_own = owner // N_SEC
    sec_own = owner % N_SEC
    local = jax.random.randint(k_local, (PAIRS,), 0, NB_DEV)
    ahead = jax.random.randint(k_step, (PAIRS,), 0, 2)
    seg_far = jnp.minimum(seg_own + ahead, N_SEG - 1)
    sec_far = jax.random.randint(k_sector, (PAIRS,), 0, N_SEC)
    sec_far = jnp.where((seg_far == seg_own) & (sec_far == sec_own), (sec_far + 1) % N_SEC, sec_far)
    target = (seg_far * N_SEC + sec_far) * NB_DEV + jax.random.randint(k_block, (PAIRS,), 0, NB_DEV)
    return jnp.stack([local, target], 1).astype(jnp.int32)


def draw_counts(key, part):
    key = jax.random.fold_in(key, 14)
    k_count, k_top = jax.random.split(key, 2)
    devices = N_SEG * N_SEC
    lowest = max(1, PAIR_DEV // 4)
    values = jax.random.randint(k_count, (devices,), lowest, PAIR_DEV + 1)
    top = jax.random.randint(k_top, (), 0, devices)
    return values.at[top].set(PAIR_DEV).astype(jnp.int32)


def plant(array, key, smallest, largest):
    longest = array.shape.index(max(array.shape))
    spots = []
    for shift in (0, 1):
        where = [jax.random.randint(jax.random.fold_in(key, axis), (), 0, length) for axis, length in enumerate(array.shape)]
        where[longest] = (where[longest] + shift) % array.shape[longest]
        spots.append(tuple(where))
    return array.at[spots[0]].set(smallest).at[spots[1]].set(largest)


def block_scale(stream_key, dims, cuts, smallest, largest):
    def one(axis_at, shards_of):
        steps = jax.random.uniform(jax.random.fold_in(jax.random.fold_in(stream_key, 6), axis_at), (shards_of,), jnp.float32, smallest / len(cuts), largest / len(cuts))
        return jnp.repeat(jnp.exp(steps), dims[axis_at] // shards_of).reshape((-1,) + (1,) * (len(dims) - axis_at - 1))

    loudness = one(*cuts[0])
    for cut in cuts[1:]:
        loudness = loudness * one(*cut)
    return loudness


def gaussian(own_key, extent, scale, bound, pieces=(), kind=jnp.bfloat16):
    factor_of = block_scale(own_key, extent, pieces, -0.22, 0.18) if pieces else 1.0
    entries = jax.random.normal(own_key, extent, jnp.float32) * scale * factor_of
    return jnp.minimum(jnp.maximum(entries, -bound), bound).astype(kind)


def setup_inputs(seed: int = 0) -> dict:
    seeds = jax.random.split(jax.random.key(seed), 9)
    theta_start = jnp.clip(0.8 + 0.40000004 * jax.random.uniform(seeds[0], (PATCHES,), jnp.float32) ** block_scale(seeds[0], (PATCHES,), ((0, 128),), -0.2, 0.2), 0.8, 1.2)
    reflect = jnp.clip(0.2 + 0.5 * jax.random.uniform(seeds[1], (BANDS, PATCHES), jnp.float32) ** block_scale(seeds[1], (BANDS, PATCHES), ((1, 128),), -0.2, 0.2), 0.2, 0.7)
    surface = draw_surface(jax.random.fold_in(seeds[8], 71), 0)
    member = draw_member(jax.random.fold_in(seeds[8], 71), 0)
    cell_map = plant(jax.random.randint(seeds[4], (PATCHES,), 0, AX * AR), jax.random.fold_in(seeds[4], 1), 0, (AX * AR) - 1).astype(jnp.int32)
    pairs = draw_pairs(jax.random.fold_in(seeds[8], 71), 0)
    counts = draw_counts(jax.random.fold_in(seeds[8], 71), 0)
    air_start = gaussian(seeds[7], (2, NAX, NAR), 0.3, 2.0, ((1, 8), (2, 16)), jnp.float32)
    return {"theta_start": theta_start, "reflect": reflect, "surface": surface, "member": member, "cell_map": cell_map, "pairs": pairs, "counts": counts, "air_start": air_start}


SOFT = 0.25
VIEW = 100.0


def kernel(geo_a, geo_b, scale):
    diff = geo_b[0:3, None, :] - geo_a[0:3, :, None]
    dist2 = jnp.sum(diff * diff, axis=0)
    cos_a = jnp.maximum(jnp.sum(geo_a[3:6, :, None] * diff, axis=0), 0.0)
    cos_b = jnp.maximum(-jnp.sum(geo_b[3:6, None, :] * diff, axis=0), 0.0)
    return (scale * cos_a * cos_b / (math.pi * (dist2 + SOFT) ** 2)).astype(jnp.bfloat16)


def air_update(air, heat, vapor):
    along = jnp.pad(air, ((0, 0), (1, 1), (0, 0)))
    cycle = jnp.concatenate([air[:, :, -1:], air, air[:, :, :1]], 2)
    lap = along[:, 2:] + along[:, :-2] + cycle[:, :, 2:] + cycle[:, :, :-2] - 4.0 * air
    source = jnp.stack([0.2 * heat, 0.2 * vapor])
    return air + 0.15 * lap - 0.3 * (air - along[:, :-2]) + source


def reference(theta_start, reflect, surface, member, cell_map, pairs, counts, air_start):
    p_dev = NB_DEV * BLK
    slots = jnp.arange(PATCHES, dtype=jnp.int32)
    order = ((slots // p_dev) * p_dev + member).astype(jnp.int32)
    geo_blk = surface[:, order].reshape(7, BLOCKS, BLK)
    rows = jnp.arange(PAIRS, dtype=jnp.int32)
    owner = rows // PAIR_DEV
    alive = ((rows % PAIR_DEV) < counts[owner]).astype(jnp.float32)
    first = (owner * NB_DEV + pairs[:, 0]).astype(jnp.int32)
    second = pairs[:, 1].astype(jnp.int32)
    scale = VIEW * NB_DEV / (PAIR_DEV * BLK)
    kernels = lax.map(lambda pair: kernel(geo_blk[:, pair[0]], geo_blk[:, pair[1]], scale), (first, second))
    device = slots // p_dev
    seg_of = device // N_SEC
    sec_of = device % N_SEC
    row_ix = seg_of * AX + cell_map // AR
    col_ix = sec_of * AR + cell_map % AR
    cell_ids = (row_ix * (N_SEC * AR) + col_ix).astype(jnp.int32)
    area = surface[6]
    absorb = 1.0 - reflect
    theta = theta_start
    air = air_start
    radiance = absorb * theta ** 4 / BANDS
    for step in range(ITERS):
        flux = (radiance * area).astype(jnp.bfloat16)
        flux_blk = flux[:, order].reshape(BANDS, BLOCKS, BLK)

        def apply(acc, item):
            kern, a, b, weight = item
            to_a = jnp.dot(flux_blk[:, b], kern.T, preferred_element_type=jnp.float32)
            to_b = jnp.dot(flux_blk[:, a], kern, preferred_element_type=jnp.float32)
            acc = acc.at[:, a].add(weight * to_a)
            acc = acc.at[:, b].add(weight * to_b)
            return acc, None

        acc, unused = lax.scan(apply, jnp.zeros((BANDS, BLOCKS, BLK), jnp.float32), (kernels, first, second, alive))
        irr = jnp.zeros((BANDS, PATCHES), jnp.float32).at[:, order].set(acc.reshape(BANDS, PATCHES))
        t_air = air[0, row_ix, col_ix]
        v_air = air[1, row_ix, col_ix]
        evap = 0.2 * (jnp.exp(theta - 1.0) - v_air)
        conv = 0.3 * (theta - t_air)
        absorbed = jnp.sum(absorb * irr, axis=0)
        emitted = theta ** 4 * jnp.sum(absorb, axis=0) / BANDS
        theta_new = theta + 0.2 * (absorbed - emitted - conv - 0.5 * evap)
        total = NAX * NAR
        heat = jax.ops.segment_sum(area * conv, cell_ids, total).reshape(NAX, NAR)
        vapor = jax.ops.segment_sum(area * evap, cell_ids, total).reshape(NAX, NAR)
        air = air_update(air, heat, vapor)
        radiance = absorb * theta_new ** 4 / BANDS + reflect * irr
        theta = theta_new
    return theta, radiance, air
```

```python
import functools
import math

import jax
import jax.numpy as jnp
from jax import lax
from jax.experimental import pallas as pl
from jax.experimental.pallas import tpu as pltpu
from jax.sharding import PartitionSpec as P

BANDS = 8
BLK = 512
NB_DEV = 2
P_DEV = NB_DEV * BLK
PAIR_DEV = 32
ITERS = 3
SOFT = 0.25
VIEW = 100.0
CELLS = 256
N_SEC = 16
SEG_BLOCKS = N_SEC * NB_DEV
SCALE = VIEW * NB_DEV / (PAIR_DEV * BLK)
CHUNK = 128
RING = 4
VMEM_LIMIT = 40 * 1024 * 1024

F32 = jnp.float32
BF16 = jnp.bfloat16
I32 = jnp.int32

REFLECT, AREA, THETA, CELL = 0, 14, 15, 16


def split3(x):
    high = x.astype(BF16).astype(F32)
    rest = x - high
    middle = rest.astype(BF16).astype(F32)
    return high, middle, rest - middle


def dot(a, b, dims=((1,), (0,))):
    return lax.dot_general(a, b, (dims, ((), ())), preferred_element_type=F32)


def exact_rows(rows, table, dims):
    count = rows.shape[0]
    parts = list(split3(rows))
    if (3 * count) % 16:
        parts.append(jnp.zeros((8, rows.shape[1]), F32))
    out = dot(jnp.concatenate(parts, 0).astype(BF16), table, dims)
    return (out[:count] + out[count : 2 * count]) + out[2 * count : 3 * count]


def slot_table(member_ref):
    patch = lax.broadcasted_iota(I32, (P_DEV, P_DEV), 0)
    return jnp.where(patch == member_ref[...], 1.0, 0.0).astype(BF16)


def fourth(theta):
    square = theta * theta
    return square * square


def arrange(theta_ref, reflect_ref, surface_ref, member_ref, cell_ref, code_ref, air_ref, state_ref, mine_ref, rows):
    rows[0:8] = reflect_ref[...]
    rows[8:15] = surface_ref[...]
    rows[15:16] = theta_ref[...]
    rows[16:17] = cell_ref[...].astype(F32)
    rows[17:32] = jnp.zeros((15, P_DEV), F32)
    state = exact_rows(rows[...], slot_table(member_ref), ((1,), (0,)))
    state_ref[...] = state[:24]
    absorb = 1.0 - state[0:8]
    radiance = absorb * fourth(state[THETA : THETA + 1]) / BANDS
    flux = (radiance * state[AREA : AREA + 1]).astype(BF16)
    mine_ref[0:6] = state[8:14]
    mine_ref[6:8] = jnp.zeros((2, P_DEV), F32)
    mine_ref[6:7, 0:128] = code_ref[...].astype(F32)
    for field in range(2):
        for row in range(2):
            start = field * CELLS + row * 128
            mine_ref[7:8, start : start + 128] = air_ref[field, row : row + 1, :]
    mine_ref[8:16] = flux.astype(F32)


def make_jobs(columns, jobs_ref, weight_v, weight_s, sem):
    far = columns[0].shape[0]
    pad = jnp.zeros((128 - far, 1), F32)
    lane = lax.broadcasted_iota(I32, (128, 128), 1)
    first = jnp.concatenate([columns[0], pad], 0)
    second = jnp.concatenate([columns[1], pad], 0)
    table = jnp.where(lane == 0, first, jnp.where(lane == 1, second, 0.0))
    weight_v[...] = table.T[0:8].astype(I32)
    copy = pltpu.make_async_copy(weight_v, weight_s, sem)
    copy.start()
    copy.wait()

    def note(at, found):
        weight = weight_s[at & 1, at >> 1]
        jobs_ref[1 + found] = at + weight * 256
        return found + jnp.where(weight > 0, 1, 0)

    found = lax.fori_loop(0, 2 * far, note, jnp.int32(0))
    jobs_ref[0] = found
    jobs_ref[1 + found] = 0
    return found


def met_by_own(codes, own, first_block, far):
    at = lax.broadcasted_iota(I32, (far, 1), 0)
    block = first_block + 2 * (at & 15) + (at >> 4)
    return jnp.sum(jnp.where(codes == (own * 256 + block).astype(F32), 1.0, 0.0), axis=1, keepdims=True)


def met_by_others(codes, target):
    return jnp.concatenate(
        [
            jnp.sum(jnp.where(codes == (side * 256 + target).astype(F32), 1.0, 0.0), axis=1, keepdims=True)
            for side in range(2)
        ],
        0,
    )


def own_factors(mine_ref, factors):
    zero = jnp.zeros((1, BLK), F32)
    one = jnp.ones((1, BLK), F32)
    for own in range(NB_DEV):
        geo = mine_ref[0:8, own * BLK : (own + 1) * BLK]
        place = [geo[i : i + 1] for i in range(3)]
        normal = [geo[i : i + 1] for i in range(3, 6)]
        along = normal[0] * place[0] + normal[1] * place[1] + normal[2] * place[2]
        square = place[0] * place[0] + place[1] * place[1] + place[2] * place[2]
        fold = SCALE / math.pi
        sets = (
            ([fold * n for n in normal] + [zero] * 5, -fold * along),
            ([zero] * 3 + place + [-one, zero], zero),
            ([-2.0 * x for x in place] + [zero] * 4 + [one], square + SOFT),
        )
        for which, (rows, constant) in enumerate(sets):
            high, middle, low = split3(jnp.concatenate(rows, 0))
            ends = jnp.concatenate(list(split3(constant)) + [zero] * 5, 0)
            full = jnp.concatenate([high, middle, low, high, middle, high, ends, jnp.zeros((8, BLK), F32)], 0)
            factors[own, :, which * BLK : (which + 1) * BLK] = full.astype(BF16)


def far_factors(geo):
    place = [geo[i : i + 1] for i in range(3)]
    normal = [geo[i : i + 1] for i in range(3, 6)]
    along = normal[0] * place[0] + normal[1] * place[1] + normal[2] * place[2]
    square = place[0] * place[0] + place[1] * place[1] + place[2] * place[2]
    row = lax.broadcasted_iota(I32, (8, BLK), 0)
    rows = jnp.where(row == 6, along, jnp.where(row == 7, square, geo))
    high, middle, low = split3(rows)
    ones = jnp.ones((8, BLK), F32)
    return jnp.concatenate([high, high, high, middle, middle, low, ones, jnp.zeros((8, BLK), F32)], 0).astype(BF16)


def job_of(code):
    at = code & 255
    far = at >> 1
    return at & 1, ((far >> 5) << 4) + (far & 15), (far >> 4) & 1, (code >> 8).astype(F32)


def build_and_apply(found, jobs_ref, far_ref, store_ref, factors, slots, sems, acc):
    def store(at, slot):
        return pltpu.make_async_copy(slots.at[slot], store_ref.at[at], sems.at[slot])

    def one(at, carry):
        slot = at & 1
        own, source, half, weight = job_of(jobs_ref[1 + at])
        lanes = pl.ds(pl.multiple_of(half * BLK, BLK), BLK)
        left = far_factors(far_ref[source, 0:8, lanes])
        flux = far_ref[source, 8:16, lanes].astype(BF16)

        @pl.when(at >= 2)
        def _():
            store(at - 2, slot).wait()

        right = factors[own]
        for start in range(0, BLK, CHUNK):
            terms = dot(left[:, start : start + CHUNK], right, ((0,), (0,)))
            near = jnp.maximum(terms[:, :BLK], 0.0)
            away = jnp.maximum(terms[:, BLK : 2 * BLK], 0.0)
            dist = terms[:, 2 * BLK :]
            slots[slot, start : start + CHUNK, :] = (near * away / (dist * dist)).astype(BF16)
        store(at, slot).start()
        acc[own] = acc[own] + weight * dot(flux, slots[slot])
        return carry

    lax.fori_loop(0, found, one, 0)
    odd = found & 1

    @pl.when(found >= 2)
    def _():
        store(found - 2, odd).wait()

    @pl.when(odd == 1)
    def _():
        slots[1] = jnp.zeros((BLK, BLK), BF16)
        store(found, 1).start()
        store(found, 1).wait()

    @pl.when(found >= 1)
    def _():
        store(found - 1, 1 - odd).wait()


def apply_stored(jobs_ref, far_ref, store_ref, slots, sems, acc):
    groups = (jobs_ref[0] + 1) >> 1

    def load(at):
        slot = at & (RING - 1)
        return pltpu.make_async_copy(store_ref.at[pl.ds(2 * at, 2)], slots.at[slot], sems.at[slot])

    for at in range(RING - 1):

        @pl.when(at < groups)
        def _(at=at):
            load(at).start()

    def one(at, carry):
        @pl.when(at + RING - 1 < groups)
        def _():
            load(at + RING - 1).start()

        load(at).wait()
        slot = at & (RING - 1)
        sums = []
        for side in range(2):
            own, source, half, weight = job_of(jobs_ref[1 + 2 * at + side])
            lanes = pl.ds(pl.multiple_of(half * BLK, BLK), BLK)
            sums.append((own, weight * dot(far_ref[source, :, lanes], slots[slot, side])[:8]))
        for own, part in sums:
            acc[own] = acc[own] + part
        return carry

    lax.fori_loop(0, groups, one, 0)


def air_rows(ref):
    return jnp.concatenate([ref[field, row : row + 1, :] for field in range(2) for row in range(2)] + [jnp.zeros((4, 128), F32)], 0)


def neighbour_air(far_ref, device):
    if far_ref.dtype == F32:
        flat = far_ref[device, 0:8, 0 : 2 * CELLS][7:8]
    else:
        rows = far_ref[device, :, 0 : 2 * CELLS].astype(F32)
        flat = (rows[8:9] + rows[9:10]) + rows[10:11]
    return jnp.concatenate([flat[:, i * 128 : (i + 1) * 128] for i in range(4)] + [jnp.zeros((4, 128), F32)], 0)


def air_step(far_ref, state_ref, theta_ref, air_ref, before_ref, after_ref, part_ref, air_out):
    seg = lax.axis_index("seg")
    sec = lax.axis_index("sec")
    theta = theta_ref[...]
    absorb = 1.0 - state_ref[0:8]
    area = state_ref[AREA : AREA + 1]
    air = air_rows(air_ref)
    fields = jnp.concatenate(
        [jnp.concatenate([air[0:1], air[1:2]], 1), jnp.concatenate([air[2:3], air[3:4]], 1), jnp.zeros((6, CELLS), F32)], 0
    )
    cell = lax.broadcasted_iota(I32, (CELLS, P_DEV), 0)
    table = jnp.where(cell == state_ref[CELL : CELL + 1].astype(I32), 1.0, 0.0).astype(BF16)
    at_patch = exact_rows(fields, table, ((1,), (0,)))
    evap = 0.2 * (jnp.exp(theta - 1.0) - at_patch[1:2])
    conv = 0.3 * (theta - at_patch[0:1])
    emitted = fourth(theta) * jnp.sum(absorb, axis=0, keepdims=True) / BANDS
    part_ref[...] = theta + 0.2 * (-emitted - conv - 0.5 * evap)
    sources = jnp.concatenate([area * conv, area * evap, jnp.zeros((6, P_DEV), F32)], 0)
    gained = exact_rows(sources, table, ((1,), (1,)))
    gain = jnp.concatenate(
        [gained[0:1, 0:128], gained[0:1, 128:256], gained[1:2, 0:128], gained[1:2, 128:256], jnp.zeros((4, 128), F32)], 0
    )
    last = lax.axis_size("seg") - 1
    before = air_rows(before_ref) * jnp.where(seg > 0, 1.0, 0.0).astype(F32)
    after = air_rows(after_ref) * jnp.where(seg < last, 1.0, 0.0).astype(F32)
    rest = jnp.zeros((4, 128), F32)
    up = jnp.concatenate([before[1:2], air[0:1], before[3:4], air[2:3], rest], 0)
    down = jnp.concatenate([air[1:2], after[0:1], air[3:4], after[2:3], rest], 0)
    lane = lax.broadcasted_iota(I32, (8, 128), 1)
    lower = neighbour_air(far_ref, (sec + N_SEC - 1) & (N_SEC - 1))
    upper = neighbour_air(far_ref, (sec + 1) & (N_SEC - 1))
    left = pltpu.roll(jnp.where(lane == 127, lower, air), 1, 1)
    right = pltpu.roll(jnp.where(lane == 0, upper, air), 127, 1)
    lap = down + up + right + left - 4.0 * air
    new = air + 0.15 * lap - 0.3 * (air - up) + 0.2 * gain
    for field in range(2):
        for row in range(2):
            air_out[field, row : row + 1, :] = new[2 * field + row : 2 * field + row + 1]


def near_first(far_ref, mine_ref, state_ref, theta_ref, air_ref, before_ref, after_ref,
               store_ref, jobs_ref, acc, part_ref, air_out,
               weight_v, weight_s, factors, slots, sems, sem):
    seg = lax.axis_index("seg")
    me = seg * N_SEC + lax.axis_index("sec")
    codes = far_ref[:, 6, 0:128]
    columns = [
        met_by_own(mine_ref[6:7, 0:128], own, seg * SEG_BLOCKS, SEG_BLOCKS) + met_by_others(codes, 2 * me + own)
        for own in range(NB_DEV)
    ]
    found = make_jobs(columns, jobs_ref, weight_v, weight_s, sem)
    own_factors(mine_ref, factors)
    acc[...] = jnp.zeros_like(acc)
    build_and_apply(found, jobs_ref, far_ref, store_ref, factors, slots, sems, acc)
    air_step(far_ref, state_ref, theta_ref, air_ref, before_ref, after_ref, part_ref, air_out)


def near_later(far_ref, store_ref, jobs_ref, state_ref, theta_ref, air_ref, before_ref, after_ref,
               acc, part_ref, air_out, slots, sems):
    acc[...] = jnp.zeros_like(acc)
    apply_stored(jobs_ref, far_ref, store_ref, slots, sems, acc)
    air_step(far_ref, state_ref, theta_ref, air_ref, before_ref, after_ref, part_ref, air_out)


def new_theta(acc, state_ref, part_ref):
    irr = jnp.concatenate([acc[0], acc[1]], 1)
    reflect = state_ref[0:8]
    absorb = 1.0 - reflect
    theta = part_ref[...] + 0.2 * jnp.sum(absorb * irr, axis=0, keepdims=True)
    return theta, absorb * fourth(theta) / BANDS + reflect * irr


def send_off(acc, state_ref, part_ref, air_ref, theta_out, out_ref):
    theta, radiance = new_theta(acc, state_ref, part_ref)
    theta_out[...] = theta
    flux = (radiance * state_ref[AREA : AREA + 1]).astype(BF16).astype(F32)
    flat = jnp.concatenate([air_ref[field, row : row + 1, :] for field in range(2) for row in range(2)], 1)
    parts = jnp.concatenate(list(split3(flat)) + [jnp.zeros((5, 2 * CELLS), F32)], 0)
    parts = jnp.concatenate([parts, jnp.zeros((8, P_DEV - 2 * CELLS), F32)], 1)
    out_ref[...] = jnp.concatenate([flux, parts], 0).astype(BF16)


def gather_far(after_ref, before_ref, far, sems):
    copies = [
        pltpu.make_async_copy(ref, far.at[pl.ds(N_SEC * i, N_SEC)], sems.at[i])
        for i, ref in enumerate((after_ref, before_ref))
    ]
    for copy in copies:
        copy.start()
    for copy in copies:
        copy.wait()


def far_first(after_ref, before_ref, mine_ref, state_ref, part_ref, air_ref, acc_in,
              store_ref, jobs_ref, theta_out, out_ref,
              acc, far, weight_v, weight_s, factors, slots, sems, sem, far_sems):
    gather_far(after_ref, before_ref, far, far_sems)
    seg = lax.axis_index("seg")
    me = seg * N_SEC + lax.axis_index("sec")
    codes = far[N_SEC : 2 * N_SEC, 6, 0:128]
    columns = [
        jnp.concatenate(
            [
                met_by_own(mine_ref[6:7, 0:128], own, (seg + 1) * SEG_BLOCKS, SEG_BLOCKS),
                met_by_others(codes, 2 * me + own),
            ],
            0,
        )
        for own in range(NB_DEV)
    ]
    found = make_jobs(columns, jobs_ref, weight_v, weight_s, sem)
    own_factors(mine_ref, factors)
    acc[...] = acc_in[...]
    build_and_apply(found, jobs_ref, far, store_ref, factors, slots, sems, acc)
    send_off(acc, state_ref, part_ref, air_ref, theta_out, out_ref)


def far_later(after_ref, before_ref, store_ref, jobs_ref, state_ref, part_ref, air_ref, acc_in,
              theta_out, out_ref, acc, far, slots, sems, far_sems):
    gather_far(after_ref, before_ref, far, far_sems)
    acc[...] = acc_in[...]
    apply_stored(jobs_ref, far, store_ref, slots, sems, acc)
    send_off(acc, state_ref, part_ref, air_ref, theta_out, out_ref)


def far_last(after_ref, before_ref, store_ref, jobs_ref, state_ref, part_ref, member_ref, acc_in,
             theta_out, out_ref, acc, far, slots, sems, far_sems):
    gather_far(after_ref, before_ref, far, far_sems)
    acc[...] = acc_in[...]
    apply_stored(jobs_ref, far, store_ref, slots, sems, acc)
    theta, radiance = new_theta(acc, state_ref, part_ref)
    rows = jnp.concatenate([radiance, theta, jnp.zeros((7, P_DEV), F32)], 0)
    back = exact_rows(rows, slot_table(member_ref), ((1,), (1,)))
    out_ref[...] = back[0:8]
    theta_out[...] = back[8:9]


VMEM = pl.BlockSpec(memory_space=pltpu.VMEM)
SMEM = pl.BlockSpec(memory_space=pltpu.SMEM)
ANY = pl.BlockSpec(memory_space=pl.ANY)


def call(body, name, ins, outs, scratch, flops):
    return pl.pallas_call(
        body,
        name=name,
        in_specs=ins,
        out_shape=[shape for shape, spec in outs],
        out_specs=[spec for shape, spec in outs],
        scratch_shapes=scratch,
        compiler_params=pltpu.CompilerParams(vmem_limit_bytes=VMEM_LIMIT),
        cost_estimate=pl.CostEstimate(flops=flops, bytes_accessed=flops // 300, transcendentals=0),
    )


def ring(value, step):
    count = lax.axis_size("seg")
    return lax.ppermute(value, "seg", [(i, (i + step) % count) for i in range(count)])


def exchange(value):
    return lax.all_to_all(jnp.broadcast_to(value[None], (N_SEC,) + value.shape), "sec", 0, 0, tiled=True)


def shards(theta_start, reflect, surface, member, cell_map, pairs, counts, air_start):
    struct = jax.ShapeDtypeStruct
    near_jobs, far_jobs = 2 * SEG_BLOCKS, 4 * SEG_BLOCKS
    row = struct((1, P_DEV), F32)
    air_like = struct((2, 2, 128), F32)
    sums = struct((NB_DEV, BANDS, BLK), F32)
    sums_buf = pltpu.VMEM((NB_DEV, BANDS, BLK), F32)
    dma = pltpu.SemaphoreType.DMA

    live = jnp.arange(PAIR_DEV, dtype=I32) < counts[0]
    code = jnp.where(live, pairs[:, 0] * 256 + pairs[:, 1], -1)
    code = jnp.concatenate([code, jnp.full((128 - PAIR_DEV,), -1, I32)])[None]
    member = member[None]
    air_before, air_after = ring(air_start, 1), ring(air_start, -1)

    state, mine = call(
        arrange, "arrange", [VMEM] * 7, [(struct((24, P_DEV), F32), VMEM), (struct((16, P_DEV), F32), VMEM)],
        [pltpu.VMEM((32, P_DEV), F32)], 10**9,
    )(theta_start[None], reflect, surface, member, cell_map[None], code, air_start)

    segment = exchange(mine)
    after, before = ring(segment, -1), ring(segment, 1)
    theta = state[THETA : THETA + 1]
    job_buf = [pltpu.VMEM((8, 128), I32), pltpu.SMEM((8, 128), I32), pltpu.VMEM((NB_DEV, 64, 3 * BLK), BF16)]
    build_buf = job_buf + [pltpu.VMEM((2, BLK, BLK), BF16), dma((2,)), dma(())]
    near_store, near_list, acc, part, air = call(
        near_first, "near_first", [VMEM] * 7,
        [(struct((near_jobs, BLK, BLK), BF16), ANY), (struct((near_jobs + 8,), I32), SMEM), (sums, VMEM), (row, VMEM), (air_like, VMEM)],
        build_buf, 10**10,
    )(segment, mine, state, theta, air_start, air_before, air_after)
    far_store, far_list, theta, out = call(
        far_first, "far_first", [ANY, ANY] + [VMEM] * 5,
        [(struct((far_jobs, BLK, BLK), BF16), ANY), (struct((far_jobs + 8,), I32), SMEM), (row, VMEM), (struct((16, P_DEV), BF16), VMEM)],
        [sums_buf, pltpu.VMEM((2 * N_SEC, 16, P_DEV), F32)] + build_buf + [dma((2,))], 10**10,
    )(after, before, mine, state, part, air, acc)

    apply_buf = [pltpu.VMEM((RING, 2, BLK, BLK), BF16), dma((RING,))]
    far_buf = [sums_buf, pltpu.VMEM((2 * N_SEC, BANDS, P_DEV), BF16)] + apply_buf + [dma((2,))]
    for step in range(1, ITERS):
        air_before, air_after = ring(air, 1), ring(air, -1)
        segment = exchange(out)
        flux = segment[:, :BANDS]
        after, before = ring(flux, -1), ring(flux, 1)
        acc, part, air = call(
            near_later, "near_later", [VMEM, ANY, SMEM] + [VMEM] * 5, [(sums, VMEM), (row, VMEM), (air_like, VMEM)], apply_buf, 5 * 10**9,
        )(segment, near_store, near_list, state, theta, air, air_before, air_after)
        if step < ITERS - 1:
            theta, out = call(
                far_later, "far_later", [ANY, ANY, ANY, SMEM] + [VMEM] * 4,
                [(row, VMEM), (struct((16, P_DEV), BF16), VMEM)], far_buf, 5 * 10**9,
            )(after, before, far_store, far_list, state, part, air, acc)
        else:
            theta, out = call(
                far_last, "far_last", [ANY, ANY, ANY, SMEM] + [VMEM] * 4,
                [(row, VMEM), (struct((BANDS, P_DEV), F32), VMEM)], far_buf, 5 * 10**9,
            )(after, before, far_store, far_list, state, part, member, acc)
    return theta[0], out, air


def solution(mesh):
    in_specs = (
        P(("seg", "sec")),
        P(None, ("seg", "sec")),
        P(None, ("seg", "sec")),
        P(("seg", "sec")),
        P(("seg", "sec")),
        P(("seg", "sec"), None),
        P(("seg", "sec")),
        P(None, "seg", "sec"),
    )
    out_specs = (P(("seg", "sec")), P(None, ("seg", "sec")), P(None, "seg", "sec"))
    return jax.shard_map(shards, mesh=mesh, in_specs=in_specs, out_specs=out_specs, check_vma=False)
```
